128 devices in a mesh: row: 8 (over z, core), col: 16 (over y, x).
Axes of the slice: x: 4, y: 4, z: 4, core: 2. Of those that a mesh axis runs over, the one named last changes fastest.
Arguments:
- p_tiles: float32 [64, 8, 2, 16, 128, 128], P(None, 'row', None, 'col'), may hold values from -0.005859375 to 0.005859375
- active: int32 [128, 8], replicated, may hold values from 0 to 511, as said below
- counts: int32 [128], P(('row', 'col')), may hold values from 1024 to 4096
- basis: bfloat16 [128, 4096, 1024], P(('row', 'col')), may hold values from -6 to 6
- kernel: float32 [128, 4096], P(('row', 'col')), may hold values from -0.09375 to 0.09375
Outputs:
- h_tiles: float32 [64, 8, 2, 16, 128, 128], P(None, 'row', None, 'col')
- density: float32 [128, 4096], P(('row', 'col'))
The draws below stay inside these ranges and needn't reach their ends.
Inputs may be any that keep to these rules, and one draw needn't show every extreme that they name: `active`: entry t of a batch's list is (s + t + 8 u_t) mod 512 for the batch's start s and u_t of 0 or 1. The tiles that the batches of one device need from one device holding them number at most 1, and every device needs exactly 1 from some holder.
All inputs are finite; a program needn't handle non-finite values.
Results may differ from the reference program's by a relative error of at most 0.0041.
Values may be sent and summed in bfloat16 or wider, within the bound.
A program may use at most 128 MiB of HBM per device.

```python
import jax
import jax.numpy as jnp
from jax import lax

TILE = 128
ACT = 8
PTS = 4096
KB = 512
BROW = 64
OGRP = 2
BATCHES = 128
N_ROW = 8
N_COL = 16


def draw_active(key, part):
    key = jax.random.fold_in(key, 11)
    first_key, second_key = jax.random.split(key)
    starts = jax.random.randint(first_key, (BATCHES,), 0, KB)
    upper = jax.random.randint(second_key, (BATCHES, ACT), 0, 2)
    steps = jnp.arange(ACT, dtype=jnp.int32)
    return ((starts[:, None] + steps[None, :] + ACT * upper) % KB).astype(jnp.int32)


def with_ends(array, own_key, smallest, high):
    dims = array.shape
    spot = [jax.random.randint(jax.random.fold_in(own_key, axis), (), 0, dims[axis]) for axis in range(len(dims))]
    array = array.at[tuple(spot)].set(smallest)
    longest = dims.index(max(dims))
    spot[longest] = (spot[longest] + 1) % dims[longest]
    return array.at[tuple(spot)].set(high)


def block_scale(stream_key, dims, cuts, smallest, top_value):
    factor_of = 1.0
    for position, shards_of in cuts:
        heights = jax.random.uniform(jax.random.fold_in(jax.random.fold_in(stream_key, 6), position), (shards_of,), jnp.float32, smallest / len(cuts), top_value / len(cuts))
        factor_of = factor_of * jnp.repeat(jnp.exp(heights), dims[position] // shards_of).reshape((-1,) + (1,) * (len(dims) - 1 - position))
    return factor_of


def bell_draw(key, shape, scale, limit, cuts=(), kind=jnp.bfloat16):
    level = block_scale(key, shape, cuts, -0.22, 0.18) if cuts else 1.0
    result = jax.random.normal(key, shape, jnp.float32) * scale * level
    return jnp.minimum(jnp.maximum(result, -limit), limit).astype(kind)


def setup_inputs(seed: int = 0) -> dict:
    keys = jax.random.split(jax.random.key(seed), 6)
    p_tiles = bell_draw(keys[0], (BROW, N_ROW, OGRP, N_COL, TILE, TILE), (ACT * ACT * TILE * TILE) ** -0.5, 0.005859375, ((1, 8), (3, 16)), jnp.float32)
    active = draw_active(jax.random.fold_in(keys[5], 71), 0)
    counts = with_ends(jax.random.randint(keys[2], (BATCHES,), PTS // 4, PTS + 1), jax.random.fold_in(keys[2], 1), PTS // 4, PTS).astype(jnp.int32)
    basis = bell_draw(keys[3], (BATCHES, PTS, ACT * TILE), 1.0, 6.0, ((0, 128),))
    kernel = bell_draw(keys[4], (BATCHES, PTS), PTS ** -0.5, 0.09375, ((0, 128),), jnp.float32)
    return dict(p_tiles=p_tiles, active=active, counts=counts, basis=basis, kernel=kernel)


def reference(p_tiles, active, counts, basis, kernel):
    slab_rows, row_count, offset_groups, col_count, tile_size, _ = p_tiles.shape
    block_total = slab_rows * row_count
    span_width = ACT * tile_size
    point_index = jnp.arange(PTS, dtype=jnp.int32)

    def one_batch(hamilton_all, inputs):
        block_list, point_count, values, kernel_row = inputs
        first_block = block_list[:, None] * jnp.ones((1, ACT), jnp.int32)
        second_block = block_list[None, :] * jnp.ones((ACT, 1), jnp.int32)
        offset = (second_block - first_block + 2 * ACT) % block_total
        slab = first_block // row_count
        row_place = first_block % row_count
        group = offset // col_count
        col_place = offset % col_count
        tiles = p_tiles[slab, row_place, group, col_place]
        matrix = tiles.astype(jnp.bfloat16).transpose(0, 2, 1, 3).reshape(span_width, span_width)
        product = jnp.dot(values, matrix, preferred_element_type=jnp.float32)
        inside = point_index < point_count
        density = jnp.where(inside, jnp.sum(product * values.astype(jnp.float32), axis=1), jnp.float32(0.0))
        weighted = ((kernel_row * density)[:, None] * values.astype(jnp.float32)).astype(jnp.bfloat16)
        hamilton = jnp.dot(values.T, weighted, preferred_element_type=jnp.float32)
        pieces = hamilton.reshape(ACT, tile_size, ACT, tile_size).transpose(0, 2, 1, 3)
        hamilton_all = hamilton_all.at[slab, row_place, group, col_place].add(pieces)
        return hamilton_all, density

    start = jnp.zeros(p_tiles.shape, jnp.float32)
    h_tiles, density = lax.scan(one_batch, start, (active, counts, basis, kernel))
    return h_tiles, density
```

```python
import functools

import jax
import jax.numpy as jnp
from jax import lax
from jax.experimental import pallas as pl
from jax.experimental.pallas import tpu as pltpu
from jax.sharding import PartitionSpec as P

MESH = pl.DeviceIdType.MESH
TILE = 128
ACT = 8
PTS = 4096
SPAN = ACT * TILE
ROWS = 8
COLS = 16
DEV = ROWS * COLS
PLACES = 128
CHUNKS = 4
CROWS = TILE // CHUNKS
UNUSED = 8
PT = 512


def exchange_kernel(
    act, cnt, kern, p_hbm, basis_hbm, dens, hrecv, table,
    p_buf, s_buf, r_buf, basis, basis_t, p_chunk, weighted, h_send, kd, slots,
    p_sem, b_sem, send_sem, recv_sem, hsend_sem, hrecv_sem, own_sem,
):
    r = lax.axis_index("row")
    c = lax.axis_index("col")
    me = r * COLS + c

    def p_copy(q):
        return pltpu.make_async_copy(p_hbm.at[:, pl.ds(q * CROWS, CROWS), :], p_buf[q], p_sem.at[q])

    def basis_copy(i):
        return pltpu.make_async_copy(basis_hbm.at[:, pl.ds(i * TILE, TILE)], basis.at[i], b_sem.at[i])

    for q in range(CHUNKS):
        p_copy(q).start()
    for i in range(ACT):
        basis_copy(i).start()

    barrier = pltpu.get_barrier_semaphore()

    def greet(d, carry):
        t = (me + d) % DEV
        pl.semaphore_signal(barrier, inc=1, device_id=(t // COLS, t % COLS), device_id_type=MESH)
        return carry

    lax.fori_loop(1, DEV, greet, 0)

    def find(n, carry):
        first = act[n * ACT]
        i = (r - first) & 7
        a = act[n * ACT + i]
        b = act[n * ACT + ((i + c) & 7)]
        o = (b - a + 2 * ACT) & 511
        place = (a >> 3) * 2 + ((o >> 4) & 1)
        table[n] = jnp.where((o & 15) == c, place, -1)
        return carry

    lax.fori_loop(0, DEV, find, 0)

    start = act[me * ACT]

    def find_slot(e, carry):
        ri = e // ACT
        rj = e % ACT
        a = act[me * ACT + ((ri - start) & 7)]
        b = act[me * ACT + ((rj - start) & 7)]
        slots[e] = ri * COLS + ((b - a + 2 * ACT) & 15)
        return carry

    lax.fori_loop(0, ACT * ACT, find_slot, 0)

    pl.semaphore_wait(barrier, DEV - 1)

    for q in range(CHUNKS):
        p_copy(q).wait()

        def pack(t, q=q):
            place = jnp.maximum(table[t], 0)
            s_buf[q][t] = p_buf[q][place].astype(jnp.bfloat16)

        @pl.when(c != UNUSED)
        def _(q=q, pack=pack):
            def send(d, carry):
                e = (d * 27) % DEV
                tr = (r + e // COLS) % ROWS
                tc = (c + e % COLS) % COLS
                t = tr * COLS + tc
                pack(t)
                pltpu.make_async_remote_copy(
                    src_ref=s_buf[q].at[t],
                    dst_ref=r_buf[q].at[me],
                    send_sem=send_sem.at[q],
                    recv_sem=recv_sem.at[q],
                    device_id=(tr, tc),
                    device_id_type=MESH,
                ).start()
                return carry

            lax.fori_loop(1, DEV, send, 0)
            pack(me)
            r_buf[q][me] = s_buf[q][me]

    for i in range(ACT):
        basis_copy(i).wait()
    for rho in range(ACT):
        block = (rho - start) & 7

        def turn(m, carry, rho=rho, block=block):
            rows = pl.ds(pl.multiple_of(m * PT, PT), PT)
            basis_t[rho, :, rows] = basis[block, rows, :].T
            return carry

        lax.fori_loop(0, PTS // PT, turn, 0)

    dens[...] = jnp.zeros_like(dens)
    for q in range(CHUNKS):
        for total, is_here in ((DEV - ROWS, c == UNUSED), (DEV - ROWS - 1, c != UNUSED)):
            @pl.when(is_here)
            def _(q=q, total=total):
                ref = r_buf[q].at[pl.ds(0, total)]
                pltpu.make_async_copy(ref, ref, recv_sem.at[q]).wait()

        def place_rows(ri, carry, q=q):
            for rj in range(ACT):
                p_chunk[ri, :, rj * TILE : (rj + 1) * TILE] = r_buf[q][slots[ri * ACT + rj]]
            return carry

        lax.fori_loop(0, ACT, place_rows, 0)

        def density_part(m, carry, q=q):
            cols = pl.ds(pl.multiple_of(m * PT, PT), PT)
            prod = jnp.dot(
                p_chunk[...].reshape(ACT * CROWS, SPAN),
                basis_t[:, :, cols].reshape(SPAN, PT),
                preferred_element_type=jnp.float32,
            )
            left = basis_t[:, q * CROWS : (q + 1) * CROWS, cols].reshape(ACT * CROWS, PT)
            dens[:, cols] += jnp.sum(prod * left.astype(jnp.float32), axis=0, keepdims=True)
            return carry

        lax.fori_loop(0, PTS // PT, density_part, 0)

    point = lax.broadcasted_iota(jnp.int32, (1, PTS), 1)
    masked = jnp.where(point < cnt[0], dens[...], 0.0)
    dens[...] = masked
    kd[...] = kern[...] * masked

    own_copy = pltpu.make_async_copy(h_send.at[0, 0], hrecv.at[me], own_sem)

    def hamilton_step(step, carry):
        pair = (step + c + c // 4) % 4

        def weigh(m, carry):
            cols = pl.ds(pl.multiple_of(m * PT, PT), PT)
            values = basis_t[pl.ds(2 * pair, 2), :, cols].reshape(2 * TILE, PT).astype(jnp.float32)
            weighted[:, cols] = (values * kd[:, cols]).astype(jnp.bfloat16)
            return carry

        lax.fori_loop(0, PTS // PT, weigh, 0)

        def part(turn_of, carry):
            m = (turn_of + r // 2 + 2 * (r % 2) + c + c // 4) % 4
            two = [basis[(2 * m + ii - start) & 7] for ii in range(2)]
            x = jnp.dot(weighted[...], jnp.concatenate(two, axis=1), preferred_element_type=jnp.float32)
            for ii in range(2):
                for jj in range(2):
                    tile = x[jj * TILE : (jj + 1) * TILE, ii * TILE : (ii + 1) * TILE]
                    h_send[2 * m + ii, 2 * pair + jj] = tile.T.astype(jnp.bfloat16)
            for ii in range(2):
                give(2 * m + ii)
            return carry

        def give(ri):
            for jj in range(2):
                rj = 2 * pair + jj
                c8 = (rj - ri + ACT) % ACT
                for half in range(2):
                    tc = c8 + half * ACT
                    is_me = jnp.logical_and(ri == r, tc == c)

                    @pl.when(jnp.logical_and(tc != UNUSED, is_me))
                    def _():
                        pltpu.make_async_copy(h_send.at[ri, rj], hrecv.at[me], own_sem).start()

                    @pl.when(jnp.logical_and(tc != UNUSED, jnp.logical_not(is_me)))
                    def _():
                        pltpu.make_async_remote_copy(
                            src_ref=h_send.at[ri, rj],
                            dst_ref=hrecv.at[me],
                            send_sem=hsend_sem,
                            recv_sem=hrecv_sem,
                            device_id=(ri, tc),
                            device_id_type=MESH,
                        ).start()

        lax.fori_loop(0, ACT // 2, part, 0)
        return carry

    lax.fori_loop(0, 4, hamilton_step, 0)

    @pl.when(c != UNUSED)
    def _():
        for q in range(CHUNKS):
            sent = s_buf[q].at[pl.ds(0, DEV - 1)]
            pltpu.make_async_copy(sent, sent, send_sem.at[q]).wait()
        own_copy.wait()
        sent = hrecv.at[pl.ds(0, DEV - ROWS - 1)]
        pltpu.make_async_copy(sent, sent, hsend_sem).wait()
        came = hrecv.at[pl.ds(0, DEV - 1)]
        pltpu.make_async_copy(came, came, hrecv_sem).wait()

    @pl.when(c == UNUSED)
    def _():
        sent = hrecv.at[pl.ds(0, DEV - ROWS)]
        pltpu.make_async_copy(sent, sent, hsend_sem).wait()


def exchange(act, cnt, kern, p, basis):
    any_space = pl.BlockSpec(memory_space=pl.ANY)
    smem = pl.BlockSpec(memory_space=pltpu.SMEM)
    vmem = pl.BlockSpec(memory_space=pltpu.VMEM)
    chunk = lambda dtype: [pltpu.VMEM((DEV, CROWS, TILE), dtype) for _ in range(CHUNKS)]
    return pl.pallas_call(
        exchange_kernel,
        out_shape=(
            jax.ShapeDtypeStruct((1, PTS), jnp.float32),
            jax.ShapeDtypeStruct((DEV, TILE, TILE), jnp.bfloat16),
            jax.ShapeDtypeStruct((DEV,), jnp.int32),
        ),
        in_specs=[smem, smem, vmem, any_space, any_space],
        out_specs=(vmem, any_space, smem),
        scratch_shapes=[
            chunk(jnp.float32),
            chunk(jnp.bfloat16),
            chunk(jnp.bfloat16),
            pltpu.VMEM((ACT, PTS, TILE), jnp.bfloat16),
            pltpu.VMEM((ACT, TILE, PTS), jnp.bfloat16),
            pltpu.VMEM((ACT, CROWS, SPAN), jnp.bfloat16),
            pltpu.VMEM((2 * TILE, PTS), jnp.bfloat16),
            pltpu.VMEM((ACT, ACT, TILE, TILE), jnp.bfloat16),
            pltpu.VMEM((1, PTS), jnp.float32),
            pltpu.SMEM((ACT * ACT,), jnp.int32),
            pltpu.SemaphoreType.DMA((CHUNKS,)),
            pltpu.SemaphoreType.DMA((ACT,)),
            pltpu.SemaphoreType.DMA((CHUNKS,)),
            pltpu.SemaphoreType.DMA((CHUNKS,)),
            pltpu.SemaphoreType.DMA,
            pltpu.SemaphoreType.DMA,
            pltpu.SemaphoreType.DMA,
        ],
        compiler_params=pltpu.CompilerParams(
            collective_id=0, has_side_effects=True, vmem_limit_bytes=56 * 2**20
        ),
    )(act, cnt, kern, p, basis)


def scatter_kernel(table, came, out):
    out[...] = jnp.zeros_like(out)

    def add(n, carry):
        place = table[n]

        @pl.when(place >= 0)
        def _():
            out[place] += came[n].astype(jnp.float32)

        return carry

    lax.fori_loop(0, DEV, add, 0)


def scatter(table, came):
    parts = 2
    rows = TILE // parts
    return pl.pallas_call(
        scatter_kernel,
        grid=(parts,),
        out_shape=jax.ShapeDtypeStruct((PLACES, TILE, TILE), jnp.float32),
        in_specs=[
            pl.BlockSpec(memory_space=pltpu.SMEM),
            pl.BlockSpec((DEV, rows, TILE), lambda g: (0, g, 0)),
        ],
        out_specs=pl.BlockSpec((PLACES, rows, TILE), lambda g: (0, g, 0)),
        compiler_params=pltpu.CompilerParams(vmem_limit_bytes=40 * 2**20),
    )(table, came)


def local(p_tiles, active, counts, basis, kernel):
    dens, came, table = exchange(
        active.reshape(DEV * ACT),
        counts,
        kernel,
        p_tiles.reshape(PLACES, TILE, TILE),
        basis.reshape(PTS, SPAN),
    )
    return scatter(table, came).reshape(p_tiles.shape), dens


def solution(mesh):
    return jax.shard_map(
        local,
        mesh=mesh,
        in_specs=(
            P(None, "row", None, "col", None, None),
            P(),
            P(("row", "col")),
            P(("row", "col"), None, None),
            P(("row", "col"), None),
        ),
        out_specs=(P(None, "row", None, "col", None, None), P(("row", "col"), None)),
        check_vma=False,
    )
```

```python
import functools

import jax
import jax.numpy as jnp
from jax import lax
from jax.experimental import pallas as pl
from jax.experimental.pallas import tpu as pltpu
from jax.sharding import PartitionSpec as P

MESH = pl.DeviceIdType.MESH
TILE = 128
ACT = 8
PTS = 4096
SPAN = ACT * TILE
ROWS = 8
COLS = 16
DEV = ROWS * COLS
PLACES = 128
SIZES = (48, 32, 32, 16)
FIRST = (0, 48, 80, 112)
CHUNKS = len(SIZES)
CROWS = 32
PARTS = TILE // CROWS
MIX = 23
EARLY = 1
UNUSED = 8
PT = 512
DPT = 1024
UNROLL = 4


def exchange_kernel(
    act, cnt, kern, p_hbm, basis_hbm, dens, hrecv, table,
    p_buf, s_buf, r_buf, basis, basis_t, p_chunk, weighted, h_send, kd, slots,
    p_sem, b_sem, send_sem, recv_sem, hsend_sem, hrecv_sem, own_sem, all_sem,
):
    r = lax.axis_index("row")
    c = lax.axis_index("col")
    me = r * COLS + c

    def p_copy(q):
        return pltpu.make_async_copy(p_hbm.at[:, pl.ds(FIRST[q], SIZES[q]), :], p_buf[q], p_sem.at[q])

    def basis_copy(i):
        return pltpu.make_async_copy(basis_hbm.at[:, pl.ds(i * TILE, TILE)], basis.at[i], b_sem.at[i])

    for q in range(CHUNKS):
        p_copy(q).start()
    for i in range(ACT):
        basis_copy(i).start()

    barrier = pltpu.get_barrier_semaphore()

    def row_peer(d):
        return lax.rem(r + d, ROWS), c

    def col_peer(d):
        return r, lax.rem(c + d, COLS)

    for d in range(1, ROWS):
        pl.semaphore_signal(barrier, inc=1, device_id=row_peer(d), device_id_type=MESH)
    for d in range(1, COLS):
        pl.semaphore_signal(barrier, inc=1, device_id=col_peer(d), device_id_type=MESH)

    def find(n, carry):
        i = (r - act[0, n]) & 7
        a = act[i, n]
        b = act[(i + c) & 7, n]
        o = (b - a + 2 * ACT) & 511
        place = (a >> 3) * 2 + ((o >> 4) & 1)
        table[n] = jnp.where((o & 15) == c, place, -1)
        return carry

    lax.fori_loop(0, DEV, find, 0)

    start = act[0, me]

    def find_slot(e, carry):
        ri = e // ACT
        rj = e % ACT
        a = act[(ri - start) & 7, me]
        b = act[(rj - start) & 7, me]
        slots[e] = ri * COLS + ((b - a + 2 * ACT) & 15)
        return carry

    lax.fori_loop(0, ACT * ACT, find_slot, 0)

    pl.semaphore_wait(barrier, ROWS + COLS - 2)
    for d in range(1, ROWS):
        pl.semaphore_signal(all_sem, inc=1, device_id=row_peer(d), device_id_type=MESH)

    def pack(q, t):
        place = jnp.maximum(table[t], 0)
        s_buf[q][t] = p_buf[q][place].astype(jnp.bfloat16)

    def send(q, tr, tc):
        t = tr * COLS + tc
        pack(q, t)
        pltpu.make_async_remote_copy(
            src_ref=s_buf[q].at[t],
            dst_ref=r_buf[q].at[me],
            send_sem=send_sem.at[q],
            recv_sem=recv_sem.at[q],
            device_id=(tr, tc),
            device_id_type=MESH,
        ).start()

    def send_to_peers(q):
        def to_row(d, carry):
            send(q, *row_peer(d))
            return carry

        def to_col(d, carry):
            send(q, *col_peer(d))
            return carry

        lax.fori_loop(1, ROWS, to_row, 0)
        lax.fori_loop(1, COLS, to_col, 0)

    def send_to_others(q):
        others = (ROWS - 1) * (COLS - 1)

        def to_other(d, carry):
            e = lax.rem(d * MIX, others)
            send(q, row_peer(1 + lax.div(e, COLS - 1))[0], col_peer(1 + lax.rem(e, COLS - 1))[1])
            return carry

        lax.fori_loop(0, others, to_other, 0)

    for q in range(EARLY):
        p_copy(q).wait()

        @pl.when(c != UNUSED)
        def _(q=q):
            send_to_peers(q)

    pl.semaphore_wait(all_sem, ROWS - 1)
    for q in range(CHUNKS):
        if q >= EARLY:
            p_copy(q).wait()

        @pl.when(c != UNUSED)
        def _(q=q):
            if q >= EARLY:
                send_to_peers(q)
            send_to_others(q)
            pack(q, me)
            r_buf[q][me] = s_buf[q][me]

    for i in range(ACT):
        basis_copy(i).wait()
    for rho in range(ACT):
        block = (rho - start) & 7

        def turn(m, carry, rho=rho, block=block):
            rows = pl.ds(pl.multiple_of(m * PT, PT), PT)
            basis_t[rho, :, rows] = basis[block, rows, :].T
            return carry

        lax.fori_loop(0, PTS // PT, turn, 0)

    dens[...] = jnp.zeros_like(dens)
    for q in range(CHUNKS):
        for total, is_here in ((DEV - ROWS, c == UNUSED), (DEV - ROWS - 1, c != UNUSED)):
            @pl.when(is_here)
            def _(q=q, total=total):
                ref = r_buf[q].at[pl.ds(0, total)]
                pltpu.make_async_copy(ref, ref, recv_sem.at[q]).wait()

        def place_rows(ri, carry, q=q):
            for rj in range(ACT):
                p_chunk[q][ri, :, rj * TILE : (rj + 1) * TILE] = r_buf[q][slots[ri * ACT + rj]]
            return carry

        lax.fori_loop(0, ACT, place_rows, 0)

        def density_part(m, carry, q=q):
            cols = pl.ds(pl.multiple_of(m * DPT, DPT), DPT)
            prod = jnp.dot(
                p_chunk[q][...].reshape(ACT * SIZES[q], SPAN),
                basis_t[:, :, cols].reshape(SPAN, DPT),
                preferred_element_type=jnp.float32,
            )
            left = basis_t[:, FIRST[q] : FIRST[q] + SIZES[q], cols].reshape(ACT * SIZES[q], DPT)
            dens[:, cols] += jnp.sum(prod * left.astype(jnp.float32), axis=0, keepdims=True)
            return carry

        lax.fori_loop(0, PTS // DPT, density_part, 0)

    point = lax.broadcasted_iota(jnp.int32, (1, PTS), 1)
    masked = jnp.where(point < cnt[0], dens[...], 0.0)
    dens[...] = masked
    kd[...] = kern[...] * masked

    own_copy = pltpu.make_async_copy(h_send.at[0, 0], hrecv.at[me], own_sem)

    def hamilton_step(step, carry):
        pair = (step + c + c // 4) % 4

        def weigh(m, carry):
            cols = pl.ds(pl.multiple_of(m * PT, PT), PT)
            values = basis_t[pl.ds(2 * pair, 2), :, cols].reshape(2 * TILE, PT).astype(jnp.float32)
            weighted[:, cols] = (values * kd[:, cols]).astype(jnp.bfloat16)
            return carry

        lax.fori_loop(0, PTS // PT, weigh, 0)

        def part(turn_of, carry):
            m = (turn_of + r // 2 + 2 * (r % 2) + c + c // 4) % 4
            two = [basis[(2 * m + ii - start) & 7] for ii in range(2)]
            x = jnp.dot(weighted[...], jnp.concatenate(two, axis=1), preferred_element_type=jnp.float32)
            for ii in range(2):
                for jj in range(2):
                    tile = x[jj * TILE : (jj + 1) * TILE, ii * TILE : (ii + 1) * TILE]
                    h_send[2 * m + ii, 2 * pair + jj] = tile.T.astype(jnp.bfloat16)
            for ii in range(2):
                give(2 * m + ii)
            return carry

        def give(ri):
            for jj in range(2):
                rj = 2 * pair + jj
                c8 = (rj - ri + ACT) % ACT
                for half in range(2):
                    tc = c8 + half * ACT
                    is_me = jnp.logical_and(ri == r, tc == c)

                    @pl.when(jnp.logical_and(tc != UNUSED, is_me))
                    def _():
                        pltpu.make_async_copy(h_send.at[ri, rj], hrecv.at[me], own_sem).start()

                    @pl.when(jnp.logical_and(tc != UNUSED, jnp.logical_not(is_me)))
                    def _():
                        pltpu.make_async_remote_copy(
                            src_ref=h_send.at[ri, rj],
                            dst_ref=hrecv.at[me],
                            send_sem=hsend_sem,
                            recv_sem=hrecv_sem,
                            device_id=(ri, tc),
                            device_id_type=MESH,
                        ).start()

        lax.fori_loop(0, ACT // 2, part, 0)
        return carry

    lax.fori_loop(0, 4, hamilton_step, 0)

    @pl.when(c != UNUSED)
    def _():
        for q in range(CHUNKS):
            sent = s_buf[q].at[pl.ds(0, DEV - 1)]
            pltpu.make_async_copy(sent, sent, send_sem.at[q]).wait()
        own_copy.wait()
        sent = hrecv.at[pl.ds(0, DEV - ROWS - 1)]
        pltpu.make_async_copy(sent, sent, hsend_sem).wait()
        came = hrecv.at[pl.ds(0, DEV - 1)]
        pltpu.make_async_copy(came, came, hrecv_sem).wait()

    @pl.when(c == UNUSED)
    def _():
        sent = hrecv.at[pl.ds(0, DEV - ROWS)]
        pltpu.make_async_copy(sent, sent, hsend_sem).wait()


def exchange(act, cnt, kern, p, basis):
    any_space = pl.BlockSpec(memory_space=pl.ANY)
    smem = pl.BlockSpec(memory_space=pltpu.SMEM)
    vmem = pl.BlockSpec(memory_space=pltpu.VMEM)
    chunk = lambda dtype: [pltpu.VMEM((DEV, rows, TILE), dtype) for rows in SIZES]
    return pl.pallas_call(
        exchange_kernel,
        out_shape=(
            jax.ShapeDtypeStruct((1, PTS), jnp.float32),
            jax.ShapeDtypeStruct((DEV, TILE, TILE), jnp.bfloat16),
            jax.ShapeDtypeStruct((DEV,), jnp.int32),
        ),
        in_specs=[smem, smem, vmem, any_space, any_space],
        out_specs=(vmem, any_space, smem),
        scratch_shapes=[
            chunk(jnp.float32),
            chunk(jnp.bfloat16),
            chunk(jnp.bfloat16),
            pltpu.VMEM((ACT, PTS, TILE), jnp.bfloat16),
            pltpu.VMEM((ACT, TILE, PTS), jnp.bfloat16),
            [pltpu.VMEM((ACT, rows, SPAN), jnp.bfloat16) for rows in SIZES],
            pltpu.VMEM((2 * TILE, PTS), jnp.bfloat16),
            pltpu.VMEM((ACT, ACT, TILE, TILE), jnp.bfloat16),
            pltpu.VMEM((1, PTS), jnp.float32),
            pltpu.SMEM((ACT * ACT,), jnp.int32),
            pltpu.SemaphoreType.DMA((CHUNKS,)),
            pltpu.SemaphoreType.DMA((ACT,)),
            pltpu.SemaphoreType.DMA((CHUNKS,)),
            pltpu.SemaphoreType.DMA((CHUNKS,)),
            pltpu.SemaphoreType.DMA,
            pltpu.SemaphoreType.DMA,
            pltpu.SemaphoreType.DMA,
            pltpu.SemaphoreType.REGULAR,
        ],
        compiler_params=pltpu.CompilerParams(
            collective_id=0, has_side_effects=True, vmem_limit_bytes=56 * 2**20
        ),
    )(act, cnt, kern, p, basis)


def scatter_kernel(table, dens, came, out, dens_out, c_buf, o_buf, which, where, in_sem, out_sem):
    def take(g):
        return pltpu.make_async_copy(came.at[:, pl.ds(g * CROWS, CROWS), :], c_buf.at[g], in_sem.at[g])

    def put(g):
        return pltpu.make_async_copy(
            o_buf.at[g, pl.ds(0, PLACES)], out.at[:, pl.ds(g * CROWS, CROWS), :], out_sem.at[g]
        )

    for g in range(PARTS):
        take(g).start()
    dens_out[...] = dens[...]

    def compact(n, count):
        place = table[n]
        which[count] = n
        where[count] = place
        return count + (place >= 0).astype(jnp.int32)

    count = lax.fori_loop(0, DEV, compact, 0)
    for e in range(UNROLL - 1):
        which[count + e] = 0
        where[count + e] = PLACES
    rounds = (count + UNROLL - 1) // UNROLL

    for g in range(PARTS):

        def clear(n, carry, g=g):
            o_buf[g, pl.ds(n * 8, 8)] = jnp.zeros((8, CROWS, TILE), jnp.float32)
            return carry

        lax.fori_loop(0, PLACES // 8, clear, 0)
        take(g).wait()

        def add(m, carry, g=g):
            for e in range(UNROLL):
                o_buf[g, where[m * UNROLL + e]] += c_buf[g, which[m * UNROLL + e]].astype(jnp.float32)
            return carry

        lax.fori_loop(0, rounds, add, 0)
        put(g).start()
    for g in range(PARTS):
        put(g).wait()


def scatter(table, dens, came):
    any_space = pl.BlockSpec(memory_space=pl.ANY)
    smem = pl.BlockSpec(memory_space=pltpu.SMEM)
    vmem = pl.BlockSpec(memory_space=pltpu.VMEM)
    return pl.pallas_call(
        scatter_kernel,
        out_shape=(
            jax.ShapeDtypeStruct((PLACES, TILE, TILE), jnp.float32),
            jax.ShapeDtypeStruct((1, PTS), jnp.float32),
        ),
        in_specs=[smem, vmem, any_space],
        out_specs=(any_space, vmem),
        scratch_shapes=[
            pltpu.VMEM((PARTS, DEV, CROWS, TILE), jnp.bfloat16),
            pltpu.VMEM((PARTS, PLACES + 1, CROWS, TILE), jnp.float32),
            pltpu.SMEM((DEV + UNROLL,), jnp.int32),
            pltpu.SMEM((DEV + UNROLL,), jnp.int32),
            pltpu.SemaphoreType.DMA((PARTS,)),
            pltpu.SemaphoreType.DMA((PARTS,)),
        ],
        compiler_params=pltpu.CompilerParams(vmem_limit_bytes=60 * 2**20),
    )(table, dens, came)


def local(p_tiles, active, counts, basis, kernel):
    dens, came, table = exchange(
        active.T,
        counts,
        kernel,
        p_tiles.reshape(PLACES, TILE, TILE),
        basis.reshape(PTS, SPAN),
    )
    h_tiles, dens = scatter(table, dens, came)
    return h_tiles.reshape(p_tiles.shape), dens


def solution(mesh):
    return jax.shard_map(
        local,
        mesh=mesh,
        in_specs=(
            P(None, "row", None, "col", None, None),
            P(),
            P(("row", "col")),
            P(("row", "col"), None, None),
            P(("row", "col"), None),
        ),
        out_specs=(P(None, "row", None, "col", None, None), P(("row", "col"), None)),
        check_vma=False,
    )
```

```python
import functools

import jax
import jax.numpy as jnp
from jax import lax
from jax.experimental import pallas as pl
from jax.experimental.pallas import tpu as pltpu
from jax.sharding import PartitionSpec as P

MESH = pl.DeviceIdType.MESH
TILE = 128
ACT = 8
PTS = 4096
SPAN = ACT * TILE
ROWS = 8
COLS = 16
DEV = ROWS * COLS
PLACES = 128
SIZES = (48, 32, 32, 16)
FIRST = (0, 48, 80, 112)
CHUNKS = len(SIZES)
CROWS = 32
PARTS = TILE // CROWS
MIX = 23
EARLY = 1
UNUSED = 8
PT = 512
DPT = 1024
UNROLL = 4


def exchange_kernel(
    act_hbm, cnt_hbm, kern_hbm, p_hbm, basis_hbm, dens_hbm, hrecv, table_hbm,
    act, cnt, kern, dens, table, p_buf, s_buf, r_buf, basis, basis_t, p_chunk, weighted, h_send, kd, slots,
    p_sem, b_sem, send_sem, recv_sem, hsend_sem, hrecv_sem, own_sem, all_sem, small_sem,
):
    r = lax.axis_index("row")
    c = lax.axis_index("col")
    me = r * COLS + c

    def p_copy(q):
        return pltpu.make_async_copy(p_hbm.at[:, pl.ds(FIRST[q], SIZES[q]), :], p_buf[q], p_sem.at[q])

    def basis_copy(i):
        return pltpu.make_async_copy(basis_hbm.at[:, pl.ds(i * TILE, TILE)], basis.at[i], b_sem.at[i])

    barrier = pltpu.get_barrier_semaphore()

    def row_peer(d):
        return lax.rem(r + d, ROWS), c

    def col_peer(d):
        return r, lax.rem(c + d, COLS)

    for d in range(1, ROWS):
        pl.semaphore_signal(barrier, inc=1, device_id=row_peer(d), device_id_type=MESH)
    for d in range(1, COLS):
        pl.semaphore_signal(barrier, inc=1, device_id=col_peer(d), device_id_type=MESH)

    act_copy = pltpu.make_async_copy(act_hbm, act, small_sem.at[0])
    cnt_copy = pltpu.make_async_copy(cnt_hbm, cnt, small_sem.at[1])
    kern_copy = pltpu.make_async_copy(kern_hbm, kern, small_sem.at[2])
    table_copy = pltpu.make_async_copy(table, table_hbm, small_sem.at[3])
    dens_copy = pltpu.make_async_copy(dens, dens_hbm, small_sem.at[4])
    act_copy.start()
    for q in range(CHUNKS):
        p_copy(q).start()
    for i in range(ACT):
        basis_copy(i).start()
    cnt_copy.start()
    kern_copy.start()
    act_copy.wait()

    def find(n, carry):
        i = (r - act[0, n]) & 7
        a = act[i, n]
        b = act[(i + c) & 7, n]
        o = (b - a + 2 * ACT) & 511
        place = (a >> 3) * 2 + ((o >> 4) & 1)
        table[n] = jnp.where((o & 15) == c, place, -1)
        return carry

    lax.fori_loop(0, DEV, find, 0)
    table_copy.start()

    start = act[0, me]

    def find_slot(e, carry):
        ri = e // ACT
        rj = e % ACT
        a = act[(ri - start) & 7, me]
        b = act[(rj - start) & 7, me]
        slots[e] = ri * COLS + ((b - a + 2 * ACT) & 15)
        return carry

    lax.fori_loop(0, ACT * ACT, find_slot, 0)

    pl.semaphore_wait(barrier, ROWS + COLS - 2)
    for d in range(1, ROWS):
        pl.semaphore_signal(all_sem, inc=1, device_id=row_peer(d), device_id_type=MESH)

    def pack(q, t):
        place = jnp.maximum(table[t], 0)
        s_buf[q][t] = p_buf[q][place].astype(jnp.bfloat16)

    def send(q, tr, tc):
        t = tr * COLS + tc
        pack(q, t)
        pltpu.make_async_remote_copy(
            src_ref=s_buf[q].at[t],
            dst_ref=r_buf[q].at[me],
            send_sem=send_sem.at[q],
            recv_sem=recv_sem.at[q],
            device_id=(tr, tc),
            device_id_type=MESH,
        ).start()

    def send_to_peers(q):
        def to_row(d, carry):
            send(q, *row_peer(d))
            return carry

        def to_col(d, carry):
            send(q, *col_peer(d))
            return carry

        lax.fori_loop(1, ROWS, to_row, 0)
        lax.fori_loop(1, COLS, to_col, 0)

    def send_to_others(q):
        others = (ROWS - 1) * (COLS - 1)

        def to_other(d, carry):
            e = lax.rem(d * MIX, others)
            send(q, row_peer(1 + lax.div(e, COLS - 1))[0], col_peer(1 + lax.rem(e, COLS - 1))[1])
            return carry

        lax.fori_loop(0, others, to_other, 0)

    for q in range(EARLY):
        p_copy(q).wait()

        @pl.when(c != UNUSED)
        def _(q=q):
            send_to_peers(q)

    pl.semaphore_wait(all_sem, ROWS - 1)
    for q in range(CHUNKS):
        if q >= EARLY:
            p_copy(q).wait()

        @pl.when(c != UNUSED)
        def _(q=q):
            if q >= EARLY:
                send_to_peers(q)
            send_to_others(q)
            pack(q, me)
            r_buf[q][me] = s_buf[q][me]

    for i in range(ACT):
        basis_copy(i).wait()
    for rho in range(ACT):
        block = (rho - start) & 7

        def turn(m, carry, rho=rho, block=block):
            rows = pl.ds(pl.multiple_of(m * PT, PT), PT)
            basis_t[rho, :, rows] = basis[block, rows, :].T
            return carry

        lax.fori_loop(0, PTS // PT, turn, 0)

    dens[...] = jnp.zeros_like(dens)
    for q in range(CHUNKS):
        for total, is_here in ((DEV - ROWS, c == UNUSED), (DEV - ROWS - 1, c != UNUSED)):
            @pl.when(is_here)
            def _(q=q, total=total):
                ref = r_buf[q].at[pl.ds(0, total)]
                pltpu.make_async_copy(ref, ref, recv_sem.at[q]).wait()

        def place_rows(ri, carry, q=q):
            for rj in range(ACT):
                p_chunk[q][ri, :, rj * TILE : (rj + 1) * TILE] = r_buf[q][slots[ri * ACT + rj]]
            return carry

        lax.fori_loop(0, ACT, place_rows, 0)

        def density_part(m, carry, q=q):
            cols = pl.ds(pl.multiple_of(m * DPT, DPT), DPT)
            prod = jnp.dot(
                p_chunk[q][...].reshape(ACT * SIZES[q], SPAN),
                basis_t[:, :, cols].reshape(SPAN, DPT),
                preferred_element_type=jnp.float32,
            )
            left = basis_t[:, FIRST[q] : FIRST[q] + SIZES[q], cols].reshape(ACT * SIZES[q], DPT)
            dens[:, cols] += jnp.sum(prod * left.astype(jnp.float32), axis=0, keepdims=True)
            return carry

        lax.fori_loop(0, PTS // DPT, density_part, 0)

    cnt_copy.wait()
    kern_copy.wait()
    point = lax.broadcasted_iota(jnp.int32, (1, PTS), 1)
    masked = jnp.where(point < cnt[0], dens[...], 0.0)
    dens[...] = masked
    dens_copy.start()
    kd[...] = kern[...] * masked

    own_copy = pltpu.make_async_copy(h_send.at[0, 0], hrecv.at[me], own_sem)

    def hamilton_step(step, carry):
        pair = (step + r // 2 + c // 4) % 4

        def weigh(m, carry):
            cols = pl.ds(pl.multiple_of(m * PT, PT), PT)
            values = basis_t[pl.ds(2 * pair, 2), :, cols].reshape(2 * TILE, PT).astype(jnp.float32)
            weighted[:, cols] = (values * kd[:, cols]).astype(jnp.bfloat16)
            return carry

        lax.fori_loop(0, PTS // PT, weigh, 0)

        def part(turn_of, carry):
            m = (turn_of + r // 2 + 2 * (r % 2) + c + c // 4) % 4
            two = [basis[(2 * m + ii - start) & 7] for ii in range(2)]
            x = jnp.dot(weighted[...], jnp.concatenate(two, axis=1), preferred_element_type=jnp.float32)
            for ii in range(2):
                for jj in range(2):
                    tile = x[jj * TILE : (jj + 1) * TILE, ii * TILE : (ii + 1) * TILE]
                    h_send[2 * m + ii, 2 * pair + jj] = tile.T.astype(jnp.bfloat16)
            for ii in range(2):
                give(2 * m + ii)
            return carry

        def give(ri):
            for jj in range(2):
                rj = 2 * pair + jj
                c8 = (rj - ri + ACT) % ACT
                for half in range(2):
                    tc = c8 + half * ACT
                    is_me = jnp.logical_and(ri == r, tc == c)

                    @pl.when(jnp.logical_and(tc != UNUSED, is_me))
                    def _():
                        pltpu.make_async_copy(h_send.at[ri, rj], hrecv.at[me], own_sem).start()

                    @pl.when(jnp.logical_and(tc != UNUSED, jnp.logical_not(is_me)))
                    def _():
                        pltpu.make_async_remote_copy(
                            src_ref=h_send.at[ri, rj],
                            dst_ref=hrecv.at[me],
                            send_sem=hsend_sem,
                            recv_sem=hrecv_sem,
                            device_id=(ri, tc),
                            device_id_type=MESH,
                        ).start()

        lax.fori_loop(0, ACT // 2, part, 0)
        return carry

    lax.fori_loop(0, 4, hamilton_step, 0)

    table_copy.wait()
    dens_copy.wait()

    @pl.when(c != UNUSED)
    def _():
        for q in range(CHUNKS):
            sent = s_buf[q].at[pl.ds(0, DEV - 1)]
            pltpu.make_async_copy(sent, sent, send_sem.at[q]).wait()
        own_copy.wait()
        sent = hrecv.at[pl.ds(0, DEV - ROWS - 1)]
        pltpu.make_async_copy(sent, sent, hsend_sem).wait()
        came = hrecv.at[pl.ds(0, DEV - 1)]
        pltpu.make_async_copy(came, came, hrecv_sem).wait()

    @pl.when(c == UNUSED)
    def _():
        sent = hrecv.at[pl.ds(0, DEV - ROWS)]
        pltpu.make_async_copy(sent, sent, hsend_sem).wait()


def exchange(act, cnt, kern, p, basis):
    any_space = pl.BlockSpec(memory_space=pl.ANY)
    chunk = lambda dtype: [pltpu.VMEM((DEV, rows, TILE), dtype) for rows in SIZES]
    return pl.pallas_call(
        exchange_kernel,
        out_shape=(
            jax.ShapeDtypeStruct((1, PTS), jnp.float32),
            jax.ShapeDtypeStruct((DEV, TILE, TILE), jnp.bfloat16),
            jax.ShapeDtypeStruct((DEV,), jnp.int32),
        ),
        in_specs=[any_space] * 5,
        out_specs=(any_space,) * 3,
        scratch_shapes=[
            pltpu.SMEM((ACT, DEV), jnp.int32),
            pltpu.SMEM((1,), jnp.int32),
            pltpu.VMEM((1, PTS), jnp.float32),
            pltpu.VMEM((1, PTS), jnp.float32),
            pltpu.SMEM((DEV,), jnp.int32),
            chunk(jnp.float32),
            chunk(jnp.bfloat16),
            chunk(jnp.bfloat16),
            pltpu.VMEM((ACT, PTS, TILE), jnp.bfloat16),
            pltpu.VMEM((ACT, TILE, PTS), jnp.bfloat16),
            [pltpu.VMEM((ACT, rows, SPAN), jnp.bfloat16) for rows in SIZES],
            pltpu.VMEM((2 * TILE, PTS), jnp.bfloat16),
            pltpu.VMEM((ACT, ACT, TILE, TILE), jnp.bfloat16),
            pltpu.VMEM((1, PTS), jnp.float32),
            pltpu.SMEM((ACT * ACT,), jnp.int32),
            pltpu.SemaphoreType.DMA((CHUNKS,)),
            pltpu.SemaphoreType.DMA((ACT,)),
            pltpu.SemaphoreType.DMA((CHUNKS,)),
            pltpu.SemaphoreType.DMA((CHUNKS,)),
            pltpu.SemaphoreType.DMA,
            pltpu.SemaphoreType.DMA,
            pltpu.SemaphoreType.DMA,
            pltpu.SemaphoreType.REGULAR,
            pltpu.SemaphoreType.DMA((5,)),
        ],
        compiler_params=pltpu.CompilerParams(
            collective_id=0, has_side_effects=True, vmem_limit_bytes=56 * 2**20
        ),
    )(act, cnt, kern, p, basis)


def scatter_kernel(
    table_hbm, dens, came, out, dens_out, table, c_buf, o_buf, which, where, in_sem, out_sem, table_sem, dens_sem
):
    table_copy = pltpu.make_async_copy(table_hbm, table, table_sem)
    dens_copy = pltpu.make_async_copy(dens, dens_out, dens_sem)
    table_copy.start()
    def take(g):
        return pltpu.make_async_copy(came.at[:, pl.ds(g * CROWS, CROWS), :], c_buf.at[g], in_sem.at[g])

    def put(g):
        return pltpu.make_async_copy(
            o_buf.at[g, pl.ds(0, PLACES)], out.at[:, pl.ds(g * CROWS, CROWS), :], out_sem.at[g]
        )

    for g in range(PARTS):
        take(g).start()
    dens_copy.start()

    def clear(n, carry):
        for g in range(PARTS):
            o_buf[g, pl.ds(n * 4, 4)] = jnp.zeros((4, CROWS, TILE), jnp.float32)
        return carry

    lax.fori_loop(0, PLACES // 4, clear, 0)
    table_copy.wait()

    def compact(n, count):
        place = table[n]
        which[count] = n
        where[count] = place
        return count + (place >= 0).astype(jnp.int32)

    count = lax.fori_loop(0, DEV, compact, 0)
    for e in range(UNROLL - 1):
        which[count + e] = 0
        where[count + e] = PLACES
    rounds = (count + UNROLL - 1) // UNROLL

    for g in range(PARTS):
        take(g).wait()

        def add(m, carry, g=g):
            for e in range(UNROLL):
                o_buf[g, where[m * UNROLL + e]] += c_buf[g, which[m * UNROLL + e]].astype(jnp.float32)
            return carry

        lax.fori_loop(0, rounds, add, 0)
        put(g).start()
    for g in range(PARTS):
        put(g).wait()
    dens_copy.wait()


def scatter(table, dens, came):
    any_space = pl.BlockSpec(memory_space=pl.ANY)
    return pl.pallas_call(
        scatter_kernel,
        out_shape=(
            jax.ShapeDtypeStruct((PLACES, TILE, TILE), jnp.float32),
            jax.ShapeDtypeStruct((1, PTS), jnp.float32),
        ),
        in_specs=[any_space] * 3,
        out_specs=(any_space,) * 2,
        scratch_shapes=[
            pltpu.SMEM((DEV,), jnp.int32),
            pltpu.VMEM((PARTS, DEV, CROWS, TILE), jnp.bfloat16),
            pltpu.VMEM((PARTS, PLACES + 1, CROWS, TILE), jnp.float32),
            pltpu.SMEM((DEV + UNROLL,), jnp.int32),
            pltpu.SMEM((DEV + UNROLL,), jnp.int32),
            pltpu.SemaphoreType.DMA((PARTS,)),
            pltpu.SemaphoreType.DMA((PARTS,)),
            pltpu.SemaphoreType.DMA,
            pltpu.SemaphoreType.DMA,
        ],
        compiler_params=pltpu.CompilerParams(vmem_limit_bytes=60 * 2**20),
    )(table, dens, came)


def local(p_tiles, active, counts, basis, kernel):
    dens, came, table = exchange(
        active.T,
        counts,
        kernel,
        p_tiles.reshape(PLACES, TILE, TILE),
        basis.reshape(PTS, SPAN),
    )
    h_tiles, dens = scatter(table, dens, came)
    return h_tiles.reshape(p_tiles.shape), dens


def solution(mesh):
    return jax.shard_map(
        local,
        mesh=mesh,
        in_specs=(
            P(None, "row", None, "col", None, None),
            P(),
            P(("row", "col")),
            P(("row", "col"), None, None),
            P(("row", "col"), None),
        ),
        out_specs=(P(None, "row", None, "col", None, None), P(("row", "col"), None)),
        check_vma=False,
    )
```

```python
import functools

import jax
import jax.numpy as jnp
from jax import lax
from jax.experimental import pallas as pl
from jax.experimental.pallas import tpu as pltpu
from jax.sharding import PartitionSpec as P

MESH = pl.DeviceIdType.MESH
TILE = 128
ACT = 8
PTS = 4096
SPAN = ACT * TILE
ROWS = 8
COLS = 16
DEV = ROWS * COLS
PLACES = 128
SIZES = (48, 32, 32, 16)
FIRST = (0, 48, 80, 112)
CHUNKS = len(SIZES)
SUM_SIZES = (16, 48, 48, 16)
SUM_FIRST = (0, 16, 64, 112)
PARTS = len(SUM_SIZES)
MIX = 23
EARLY = 1
UNUSED = 8
PT = 512
DPT = 1024
UNROLL = 4


def exchange_kernel(
    act_hbm, cnt_hbm, kern_hbm, p_hbm, basis_hbm, dens_hbm, hrecv, table_hbm,
    act, cnt, kern, dens, table, p_buf, s_buf, r_buf, basis, basis_t, p_chunk, weighted, h_send, kd, slots,
    p_sem, b_sem, send_sem, recv_sem, hsend_sem, hrecv_sem, own_sem, all_sem, small_sem,
):
    r = lax.axis_index("row")
    c = lax.axis_index("col")
    me = r * COLS + c

    def p_copy(q):
        return pltpu.make_async_copy(p_hbm.at[:, pl.ds(FIRST[q], SIZES[q]), :], p_buf[q], p_sem.at[q])

    def basis_copy(i):
        return pltpu.make_async_copy(basis_hbm.at[:, pl.ds(i * TILE, TILE)], basis.at[i], b_sem.at[i])

    barrier = pltpu.get_barrier_semaphore()

    def row_peer(d):
        return lax.rem(r + d, ROWS), c

    def col_peer(d):
        return r, lax.rem(c + d, COLS)

    for d in range(1, ROWS):
        pl.semaphore_signal(barrier, inc=1, device_id=row_peer(d), device_id_type=MESH)
    for d in range(1, COLS):
        pl.semaphore_signal(barrier, inc=1, device_id=col_peer(d), device_id_type=MESH)

    act_copy = pltpu.make_async_copy(act_hbm, act, small_sem.at[0])
    cnt_copy = pltpu.make_async_copy(cnt_hbm, cnt, small_sem.at[1])
    kern_copy = pltpu.make_async_copy(kern_hbm, kern, small_sem.at[2])
    table_copy = pltpu.make_async_copy(table, table_hbm, small_sem.at[3])
    dens_copy = pltpu.make_async_copy(dens, dens_hbm, small_sem.at[4])
    act_copy.start()
    for q in range(CHUNKS):
        p_copy(q).start()
    for i in range(ACT):
        basis_copy(i).start()
    cnt_copy.start()
    kern_copy.start()
    act_copy.wait()

    def find(n, carry):
        i = (r - act[0, n]) & 7
        a = act[i, n]
        b = act[(i + c) & 7, n]
        o = (b - a + 2 * ACT) & 511
        place = (a >> 3) * 2 + ((o >> 4) & 1)
        table[n] = jnp.where((o & 15) == c, place, -1)
        return carry

    lax.fori_loop(0, DEV, find, 0)
    table_copy.start()

    start = act[0, me]

    def find_slot(e, carry):
        ri = e // ACT
        rj = e % ACT
        a = act[(ri - start) & 7, me]
        b = act[(rj - start) & 7, me]
        slots[e] = ri * COLS + ((b - a + 2 * ACT) & 15)
        return carry

    lax.fori_loop(0, ACT * ACT, find_slot, 0)

    pl.semaphore_wait(barrier, ROWS + COLS - 2)
    for d in range(1, ROWS):
        pl.semaphore_signal(all_sem, inc=1, device_id=row_peer(d), device_id_type=MESH)

    def pack(q, t):
        place = jnp.maximum(table[t], 0)
        s_buf[q][t] = p_buf[q][place].astype(jnp.bfloat16)

    def send(q, tr, tc):
        t = tr * COLS + tc
        pack(q, t)
        pltpu.make_async_remote_copy(
            src_ref=s_buf[q].at[t],
            dst_ref=r_buf[q].at[me],
            send_sem=send_sem.at[q],
            recv_sem=recv_sem.at[q],
            device_id=(tr, tc),
            device_id_type=MESH,
        ).start()

    def send_to_peers(q):
        def to_row(d, carry):
            send(q, *row_peer(d))
            return carry

        def to_col(d, carry):
            send(q, *col_peer(d))
            return carry

        lax.fori_loop(1, ROWS, to_row, 0)
        lax.fori_loop(1, COLS, to_col, 0)

    def send_to_others(q):
        others = (ROWS - 1) * (COLS - 1)

        def to_other(d, carry):
            e = lax.rem(d * MIX, others)
            send(q, row_peer(1 + lax.div(e, COLS - 1))[0], col_peer(1 + lax.rem(e, COLS - 1))[1])
            return carry

        lax.fori_loop(0, others, to_other, 0)

    for q in range(EARLY):
        p_copy(q).wait()

        @pl.when(c != UNUSED)
        def _(q=q):
            send_to_peers(q)

    pl.semaphore_wait(all_sem, ROWS - 1)
    for q in range(CHUNKS):
        if q >= EARLY:
            p_copy(q).wait()

        @pl.when(c != UNUSED)
        def _(q=q):
            send_to_others(q)
            if q >= EARLY:
                send_to_peers(q)
            pack(q, me)
            r_buf[q][me] = s_buf[q][me]

    for i in range(ACT):
        basis_copy(i).wait()
    for rho in range(ACT):
        block = (rho - start) & 7

        def turn(m, carry, rho=rho, block=block):
            rows = pl.ds(pl.multiple_of(m * PT, PT), PT)
            basis_t[rho, :, rows] = basis[block, rows, :].T
            return carry

        lax.fori_loop(0, PTS // PT, turn, 0)

    dens[...] = jnp.zeros_like(dens)
    for q in range(CHUNKS):
        for total, is_here in ((DEV - ROWS, c == UNUSED), (DEV - ROWS - 1, c != UNUSED)):
            @pl.when(is_here)
            def _(q=q, total=total):
                ref = r_buf[q].at[pl.ds(0, total)]
                pltpu.make_async_copy(ref, ref, recv_sem.at[q]).wait()

        def place_rows(ri, carry, q=q):
            for rj in range(ACT):
                p_chunk[q][ri, :, rj * TILE : (rj + 1) * TILE] = r_buf[q][slots[ri * ACT + rj]]
            return carry

        lax.fori_loop(0, ACT, place_rows, 0)

        def density_part(m, carry, q=q):
            cols = pl.ds(pl.multiple_of(m * DPT, DPT), DPT)
            prod = jnp.dot(
                p_chunk[q][...].reshape(ACT * SIZES[q], SPAN),
                basis_t[:, :, cols].reshape(SPAN, DPT),
                preferred_element_type=jnp.float32,
            )
            left = basis_t[:, FIRST[q] : FIRST[q] + SIZES[q], cols].reshape(ACT * SIZES[q], DPT)
            dens[:, cols] += jnp.sum(prod * left.astype(jnp.float32), axis=0, keepdims=True)
            return carry

        lax.fori_loop(0, PTS // DPT, density_part, 0)

    cnt_copy.wait()
    kern_copy.wait()
    point = lax.broadcasted_iota(jnp.int32, (1, PTS), 1)
    masked = jnp.where(point < cnt[0], dens[...], 0.0)
    dens[...] = masked
    dens_copy.start()
    kd[...] = kern[...] * masked

    own_copy = pltpu.make_async_copy(h_send.at[0, 0], hrecv.at[me], own_sem)

    def hamilton_step(step, carry):
        pair = (step + r // 2 + c // 4) % 4

        def weigh(m, carry):
            cols = pl.ds(pl.multiple_of(m * PT, PT), PT)
            values = basis_t[pl.ds(2 * pair, 2), :, cols].reshape(2 * TILE, PT).astype(jnp.float32)
            weighted[:, cols] = (values * kd[:, cols]).astype(jnp.bfloat16)
            return carry

        lax.fori_loop(0, PTS // PT, weigh, 0)

        def part(turn_of, carry):
            m = (3 * turn_of + r // 2 + 2 * (r % 2) + c + c // 4) % 4
            two = [basis[(2 * m + ii - start) & 7] for ii in range(2)]
            x = jnp.dot(weighted[...], jnp.concatenate(two, axis=1), preferred_element_type=jnp.float32)
            for ii in range(2):
                for jj in range(2):
                    tile = x[jj * TILE : (jj + 1) * TILE, ii * TILE : (ii + 1) * TILE]
                    h_send[2 * m + ii, 2 * pair + jj] = tile.T.astype(jnp.bfloat16)
            for ii in range(2):
                give(2 * m + ii)
            return carry

        def give(ri):
            for jj in range(2):
                rj = 2 * pair + jj
                c8 = (rj - ri + ACT) % ACT
                for half in range(2):
                    tc = c8 + half * ACT
                    is_me = jnp.logical_and(ri == r, tc == c)

                    @pl.when(jnp.logical_and(tc != UNUSED, is_me))
                    def _():
                        pltpu.make_async_copy(h_send.at[ri, rj], hrecv.at[me], own_sem).start()

                    @pl.when(jnp.logical_and(tc != UNUSED, jnp.logical_not(is_me)))
                    def _():
                        pltpu.make_async_remote_copy(
                            src_ref=h_send.at[ri, rj],
                            dst_ref=hrecv.at[me],
                            send_sem=hsend_sem,
                            recv_sem=hrecv_sem,
                            device_id=(ri, tc),
                            device_id_type=MESH,
                        ).start()

        lax.fori_loop(0, ACT // 2, part, 0)
        return carry

    lax.fori_loop(0, 4, hamilton_step, 0)

    table_copy.wait()
    dens_copy.wait()

    @pl.when(c != UNUSED)
    def _():
        for q in range(CHUNKS):
            sent = s_buf[q].at[pl.ds(0, DEV - 1)]
            pltpu.make_async_copy(sent, sent, send_sem.at[q]).wait()
        own_copy.wait()
        sent = hrecv.at[pl.ds(0, DEV - ROWS - 1)]
        pltpu.make_async_copy(sent, sent, hsend_sem).wait()
        came = hrecv.at[pl.ds(0, DEV - 1)]
        pltpu.make_async_copy(came, came, hrecv_sem).wait()

    @pl.when(c == UNUSED)
    def _():
        sent = hrecv.at[pl.ds(0, DEV - ROWS)]
        pltpu.make_async_copy(sent, sent, hsend_sem).wait()


def exchange(act, cnt, kern, p, basis):
    any_space = pl.BlockSpec(memory_space=pl.ANY)
    chunk = lambda dtype: [pltpu.VMEM((DEV, rows, TILE), dtype) for rows in SIZES]
    return pl.pallas_call(
        exchange_kernel,
        out_shape=(
            jax.ShapeDtypeStruct((1, PTS), jnp.float32),
            jax.ShapeDtypeStruct((DEV, TILE, TILE), jnp.bfloat16),
            jax.ShapeDtypeStruct((DEV,), jnp.int32),
        ),
        in_specs=[any_space] * 5,
        out_specs=(any_space,) * 3,
        scratch_shapes=[
            pltpu.SMEM((ACT, DEV), jnp.int32),
            pltpu.SMEM((1,), jnp.int32),
            pltpu.VMEM((1, PTS), jnp.float32),
            pltpu.VMEM((1, PTS), jnp.float32),
            pltpu.SMEM((DEV,), jnp.int32),
            chunk(jnp.float32),
            chunk(jnp.bfloat16),
            chunk(jnp.bfloat16),
            pltpu.VMEM((ACT, PTS, TILE), jnp.bfloat16),
            pltpu.VMEM((ACT, TILE, PTS), jnp.bfloat16),
            [pltpu.VMEM((ACT, rows, SPAN), jnp.bfloat16) for rows in SIZES],
            pltpu.VMEM((2 * TILE, PTS), jnp.bfloat16),
            pltpu.VMEM((ACT, ACT, TILE, TILE), jnp.bfloat16),
            pltpu.VMEM((1, PTS), jnp.float32),
            pltpu.SMEM((ACT * ACT,), jnp.int32),
            pltpu.SemaphoreType.DMA((CHUNKS,)),
            pltpu.SemaphoreType.DMA((ACT,)),
            pltpu.SemaphoreType.DMA((CHUNKS,)),
            pltpu.SemaphoreType.DMA((CHUNKS,)),
            pltpu.SemaphoreType.DMA,
            pltpu.SemaphoreType.DMA,
            pltpu.SemaphoreType.DMA,
            pltpu.SemaphoreType.REGULAR,
            pltpu.SemaphoreType.DMA((5,)),
        ],
        compiler_params=pltpu.CompilerParams(
            collective_id=0, has_side_effects=True, vmem_limit_bytes=56 * 2**20
        ),
    )(act, cnt, kern, p, basis)


def scatter_kernel(
    table_hbm, dens, came, out, dens_out, table, c_buf, o_buf, which, where, in_sem, out_sem, table_sem, dens_sem
):
    table_copy = pltpu.make_async_copy(table_hbm, table, table_sem)
    dens_copy = pltpu.make_async_copy(dens, dens_out, dens_sem)
    table_copy.start()
    def take(g):
        return pltpu.make_async_copy(came.at[:, pl.ds(SUM_FIRST[g], SUM_SIZES[g]), :], c_buf[g], in_sem.at[g])

    def put(g):
        return pltpu.make_async_copy(
            o_buf[g].at[pl.ds(0, PLACES)], out.at[:, pl.ds(SUM_FIRST[g], SUM_SIZES[g]), :], out_sem.at[g]
        )

    for g in range(PARTS):
        take(g).start()
    dens_copy.start()

    def clear(n, carry):
        for g in range(PARTS):
            o_buf[g][pl.ds(n * 4, 4)] = jnp.zeros((4, SUM_SIZES[g], TILE), jnp.float32)
        return carry

    lax.fori_loop(0, PLACES // 4, clear, 0)
    table_copy.wait()

    def compact(n, count):
        place = table[n]
        which[count] = n
        where[count] = place
        return count + (place >= 0).astype(jnp.int32)

    count = lax.fori_loop(0, DEV, compact, 0)
    for e in range(UNROLL - 1):
        which[count + e] = 0
        where[count + e] = PLACES
    rounds = (count + UNROLL - 1) // UNROLL

    for g in range(PARTS):
        take(g).wait()

        def add(m, carry, g=g):
            for e in range(UNROLL):
                o_buf[g][where[m * UNROLL + e]] += c_buf[g][which[m * UNROLL + e]].astype(jnp.float32)
            return carry

        lax.fori_loop(0, rounds, add, 0)
        put(g).start()
    for g in range(PARTS):
        put(g).wait()
    dens_copy.wait()


def scatter(table, dens, came):
    any_space = pl.BlockSpec(memory_space=pl.ANY)
    return pl.pallas_call(
        scatter_kernel,
        out_shape=(
            jax.ShapeDtypeStruct((PLACES, TILE, TILE), jnp.float32),
            jax.ShapeDtypeStruct((1, PTS), jnp.float32),
        ),
        in_specs=[any_space] * 3,
        out_specs=(any_space,) * 2,
        scratch_shapes=[
            pltpu.SMEM((DEV,), jnp.int32),
            [pltpu.VMEM((DEV, rows, TILE), jnp.bfloat16) for rows in SUM_SIZES],
            [pltpu.VMEM((PLACES + 1, rows, TILE), jnp.float32) for rows in SUM_SIZES],
            pltpu.SMEM((DEV + UNROLL,), jnp.int32),
            pltpu.SMEM((DEV + UNROLL,), jnp.int32),
            pltpu.SemaphoreType.DMA((PARTS,)),
            pltpu.SemaphoreType.DMA((PARTS,)),
            pltpu.SemaphoreType.DMA,
            pltpu.SemaphoreType.DMA,
        ],
        compiler_params=pltpu.CompilerParams(vmem_limit_bytes=60 * 2**20),
    )(table, dens, came)


def local(p_tiles, active, counts, basis, kernel):
    dens, came, table = exchange(
        active.T,
        counts,
        kernel,
        p_tiles.reshape(PLACES, TILE, TILE),
        basis.reshape(PTS, SPAN),
    )
    h_tiles, dens = scatter(table, dens, came)
    return h_tiles.reshape(p_tiles.shape), dens


def solution(mesh):
    return jax.shard_map(
        local,
        mesh=mesh,
        in_specs=(
            P(None, "row", None, "col", None, None),
            P(),
            P(("row", "col")),
            P(("row", "col"), None, None),
            P(("row", "col"), None),
        ),
        out_specs=(P(None, "row", None, "col", None, None), P(("row", "col"), None)),
        check_vma=False,
    )
```

```python
import functools

import jax
import jax.numpy as jnp
from jax import lax
from jax.experimental import pallas as pl
from jax.experimental.pallas import tpu as pltpu
from jax.sharding import PartitionSpec as P

MESH = pl.DeviceIdType.MESH
TILE = 128
ACT = 8
PTS = 4096
SPAN = ACT * TILE
ROWS = 8
COLS = 16
DEV = ROWS * COLS
PLACES = 128
SIZES = (48, 32, 32, 16)
FIRST = (0, 48, 80, 112)
CHUNKS = len(SIZES)
SUM_SIZES = (16, 48, 48, 16)
SUM_FIRST = (0, 16, 64, 112)
PARTS = len(SUM_SIZES)
MIX = 23
EARLY = 1
UNUSED = 8
PT = 1024
DPT = 2048
UNROLL = 4


def exchange_kernel(
    act_hbm, cnt_hbm, kern_hbm, p_hbm, basis_hbm, dens_hbm, hrecv, table_hbm,
    act, cnt, kern, dens, table, p_buf, s_buf, r_buf, basis, basis_t, p_chunk, weighted, h_send, kd, slots,
    p_sem, b_sem, send_sem, recv_sem, hsend_sem, hrecv_sem, own_sem, all_sem, small_sem,
):
    r = lax.axis_index("row")
    c = lax.axis_index("col")
    me = r * COLS + c

    def p_copy(q):
        return pltpu.make_async_copy(p_hbm.at[:, pl.ds(FIRST[q], SIZES[q]), :], p_buf[q], p_sem.at[q])

    def basis_copy(i):
        return pltpu.make_async_copy(basis_hbm.at[:, pl.ds(i * TILE, TILE)], basis.at[i], b_sem.at[i])

    barrier = pltpu.get_barrier_semaphore()

    def row_peer(d):
        return lax.rem(r + d, ROWS), c

    def col_peer(d):
        return r, lax.rem(c + d, COLS)

    for d in range(1, ROWS):
        pl.semaphore_signal(barrier, inc=1, device_id=row_peer(d), device_id_type=MESH)
    for d in range(1, COLS):
        pl.semaphore_signal(barrier, inc=1, device_id=col_peer(d), device_id_type=MESH)

    act_copy = pltpu.make_async_copy(act_hbm, act, small_sem.at[0])
    cnt_copy = pltpu.make_async_copy(cnt_hbm, cnt, small_sem.at[1])
    kern_copy = pltpu.make_async_copy(kern_hbm, kern, small_sem.at[2])
    table_copy = pltpu.make_async_copy(table, table_hbm, small_sem.at[3])
    dens_copy = pltpu.make_async_copy(dens, dens_hbm, small_sem.at[4])
    act_copy.start()
    for q in range(CHUNKS):
        p_copy(q).start()
    for i in range(ACT):
        basis_copy(i).start()
    cnt_copy.start()
    kern_copy.start()
    act_copy.wait()

    def find(n, carry):
        i = (r - act[0, n]) & 7
        a = act[i, n]
        b = act[(i + c) & 7, n]
        o = (b - a + 2 * ACT) & 511
        place = (a >> 3) * 2 + ((o >> 4) & 1)
        table[n] = jnp.where((o & 15) == c, place, -1)
        return carry

    lax.fori_loop(0, DEV, find, 0)
    table_copy.start()

    start = act[0, me]

    def find_slot(e, carry):
        ri = e // ACT
        rj = e % ACT
        a = act[(ri - start) & 7, me]
        b = act[(rj - start) & 7, me]
        slots[e] = ri * COLS + ((b - a + 2 * ACT) & 15)
        return carry

    lax.fori_loop(0, ACT * ACT, find_slot, 0)

    pl.semaphore_wait(barrier, ROWS + COLS - 2)
    for d in range(1, ROWS):
        pl.semaphore_signal(all_sem, inc=1, device_id=row_peer(d), device_id_type=MESH)

    def pack(q, t):
        place = jnp.maximum(table[t], 0)
        s_buf[q][t] = p_buf[q][place].astype(jnp.bfloat16)

    def send(q, tr, tc):
        t = tr * COLS + tc
        pack(q, t)
        pltpu.make_async_remote_copy(
            src_ref=s_buf[q].at[t],
            dst_ref=r_buf[q].at[me],
            send_sem=send_sem.at[q],
            recv_sem=recv_sem.at[q],
            device_id=(tr, tc),
            device_id_type=MESH,
        ).start()

    def send_to_peers(q):
        def to_row(d, carry):
            send(q, *row_peer(d))
            return carry

        def to_col(d, carry):
            send(q, *col_peer(d))
            return carry

        lax.fori_loop(1, ROWS, to_row, 0)
        lax.fori_loop(1, COLS, to_col, 0)

    def send_to_others(q):
        others = (ROWS - 1) * (COLS - 1)

        def to_other(d, carry):
            e = lax.rem(d * MIX, others)
            send(q, row_peer(1 + lax.div(e, COLS - 1))[0], col_peer(1 + lax.rem(e, COLS - 1))[1])
            return carry

        lax.fori_loop(0, others, to_other, 0)

    for q in range(EARLY):
        p_copy(q).wait()

        @pl.when(c != UNUSED)
        def _(q=q):
            send_to_peers(q)

    pl.semaphore_wait(all_sem, ROWS - 1)
    for q in range(CHUNKS):
        if q >= EARLY:
            p_copy(q).wait()

        @pl.when(c != UNUSED)
        def _(q=q):
            send_to_others(q)
            if q >= EARLY:
                send_to_peers(q)
            pack(q, me)
            r_buf[q][me] = s_buf[q][me]

    for i in range(ACT):
        basis_copy(i).wait()
    for rho in range(ACT):
        block = (rho - start) & 7

        def turn(m, carry, rho=rho, block=block):
            rows = pl.ds(pl.multiple_of(m * PT, PT), PT)
            basis_t[rho, :, rows] = basis[block, rows, :].T
            return carry

        lax.fori_loop(0, PTS // PT, turn, 0)

    dens[...] = jnp.zeros_like(dens)
    for q in range(CHUNKS):
        for total, is_here in ((DEV - ROWS, c == UNUSED), (DEV - ROWS - 1, c != UNUSED)):
            @pl.when(is_here)
            def _(q=q, total=total):
                ref = r_buf[q].at[pl.ds(0, total)]
                pltpu.make_async_copy(ref, ref, recv_sem.at[q]).wait()

        def place_rows(ri, carry, q=q):
            for rj in range(ACT):
                p_chunk[q][ri, :, rj * TILE : (rj + 1) * TILE] = r_buf[q][slots[ri * ACT + rj]]
            return carry

        lax.fori_loop(0, ACT, place_rows, 0)

        def density_part(m, carry, q=q):
            cols = pl.ds(pl.multiple_of(m * DPT, DPT), DPT)
            prod = jnp.dot(
                p_chunk[q][...].reshape(ACT * SIZES[q], SPAN),
                basis_t[:, :, cols].reshape(SPAN, DPT),
                preferred_element_type=jnp.float32,
            )
            left = basis_t[:, FIRST[q] : FIRST[q] + SIZES[q], cols].reshape(ACT * SIZES[q], DPT)
            dens[:, cols] += jnp.sum(prod * left.astype(jnp.float32), axis=0, keepdims=True)
            return carry

        lax.fori_loop(0, PTS // DPT, density_part, 0)

    cnt_copy.wait()
    kern_copy.wait()
    point = lax.broadcasted_iota(jnp.int32, (1, PTS), 1)
    masked = jnp.where(point < cnt[0], dens[...], 0.0)
    dens[...] = masked
    dens_copy.start()
    kd[...] = kern[...] * masked

    own_copy = pltpu.make_async_copy(h_send.at[0, 0], hrecv.at[me], own_sem)

    def hamilton_step(step, carry):
        pair = (step + r // 2 + c // 4) % 4

        def weigh(m, carry):
            cols = pl.ds(pl.multiple_of(m * PT, PT), PT)
            values = basis_t[pl.ds(2 * pair, 2), :, cols].reshape(2 * TILE, PT).astype(jnp.float32)
            weighted[:, cols] = (values * kd[:, cols]).astype(jnp.bfloat16)
            return carry

        lax.fori_loop(0, PTS // PT, weigh, 0)

        def part(turn_of, carry):
            m = (3 * turn_of + r // 2 + 2 * (r % 2) + c + c // 4) % 4
            two = [basis[(2 * m + ii - start) & 7] for ii in range(2)]
            x = jnp.dot(weighted[...], jnp.concatenate(two, axis=1), preferred_element_type=jnp.float32)
            for ii in range(2):
                for jj in range(2):
                    tile = x[jj * TILE : (jj + 1) * TILE, ii * TILE : (ii + 1) * TILE]
                    h_send[2 * m + ii, 2 * pair + jj] = tile.astype(jnp.bfloat16).T
            for ii in range(2):
                give(2 * m + ii)
            return carry

        def give(ri):
            for jj in range(2):
                rj = 2 * pair + jj
                c8 = (rj - ri + ACT) % ACT
                for half in range(2):
                    tc = c8 + half * ACT
                    is_me = jnp.logical_and(ri == r, tc == c)

                    @pl.when(jnp.logical_and(tc != UNUSED, is_me))
                    def _():
                        pltpu.make_async_copy(h_send.at[ri, rj], hrecv.at[me], own_sem).start()

                    @pl.when(jnp.logical_and(tc != UNUSED, jnp.logical_not(is_me)))
                    def _():
                        pltpu.make_async_remote_copy(
                            src_ref=h_send.at[ri, rj],
                            dst_ref=hrecv.at[me],
                            send_sem=hsend_sem,
                            recv_sem=hrecv_sem,
                            device_id=(ri, tc),
                            device_id_type=MESH,
                        ).start()

        lax.fori_loop(0, ACT // 2, part, 0)
        return carry

    lax.fori_loop(0, 4, hamilton_step, 0)

    table_copy.wait()
    dens_copy.wait()

    @pl.when(c != UNUSED)
    def _():
        for q in range(CHUNKS):
            sent = s_buf[q].at[pl.ds(0, DEV - 1)]
            pltpu.make_async_copy(sent, sent, send_sem.at[q]).wait()
        own_copy.wait()
        sent = hrecv.at[pl.ds(0, DEV - ROWS - 1)]
        pltpu.make_async_copy(sent, sent, hsend_sem).wait()
        came = hrecv.at[pl.ds(0, DEV - 1)]
        pltpu.make_async_copy(came, came, hrecv_sem).wait()

    @pl.when(c == UNUSED)
    def _():
        sent = hrecv.at[pl.ds(0, DEV - ROWS)]
        pltpu.make_async_copy(sent, sent, hsend_sem).wait()


def exchange(act, cnt, kern, p, basis):
    any_space = pl.BlockSpec(memory_space=pl.ANY)
    chunk = lambda dtype: [pltpu.VMEM((DEV, rows, TILE), dtype) for rows in SIZES]
    return pl.pallas_call(
        exchange_kernel,
        out_shape=(
            jax.ShapeDtypeStruct((1, PTS), jnp.float32),
            jax.ShapeDtypeStruct((DEV, TILE, TILE), jnp.bfloat16),
            jax.ShapeDtypeStruct((DEV,), jnp.int32),
        ),
        in_specs=[any_space] * 5,
        out_specs=(any_space,) * 3,
        scratch_shapes=[
            pltpu.SMEM((ACT, DEV), jnp.int32),
            pltpu.SMEM((1,), jnp.int32),
            pltpu.VMEM((1, PTS), jnp.float32),
            pltpu.VMEM((1, PTS), jnp.float32),
            pltpu.SMEM((DEV,), jnp.int32),
            chunk(jnp.float32),
            chunk(jnp.bfloat16),
            chunk(jnp.bfloat16),
            pltpu.VMEM((ACT, PTS, TILE), jnp.bfloat16),
            pltpu.VMEM((ACT, TILE, PTS), jnp.bfloat16),
            [pltpu.VMEM((ACT, rows, SPAN), jnp.bfloat16) for rows in SIZES],
            pltpu.VMEM((2 * TILE, PTS), jnp.bfloat16),
            pltpu.VMEM((ACT, ACT, TILE, TILE), jnp.bfloat16),
            pltpu.VMEM((1, PTS), jnp.float32),
            pltpu.SMEM((ACT * ACT,), jnp.int32),
            pltpu.SemaphoreType.DMA((CHUNKS,)),
            pltpu.SemaphoreType.DMA((ACT,)),
            pltpu.SemaphoreType.DMA((CHUNKS,)),
            pltpu.SemaphoreType.DMA((CHUNKS,)),
            pltpu.SemaphoreType.DMA,
            pltpu.SemaphoreType.DMA,
            pltpu.SemaphoreType.DMA,
            pltpu.SemaphoreType.REGULAR,
            pltpu.SemaphoreType.DMA((5,)),
        ],
        compiler_params=pltpu.CompilerParams(
            collective_id=0, has_side_effects=True, vmem_limit_bytes=56 * 2**20
        ),
    )(act, cnt, kern, p, basis)


def scatter_kernel(
    table_hbm, dens, came, out, dens_out, table, c_buf, o_buf, which, where, in_sem, out_sem, table_sem, dens_sem
):
    table_copy = pltpu.make_async_copy(table_hbm, table, table_sem)
    dens_copy = pltpu.make_async_copy(dens, dens_out, dens_sem)
    table_copy.start()
    def take(g):
        return pltpu.make_async_copy(came.at[:, pl.ds(SUM_FIRST[g], SUM_SIZES[g]), :], c_buf[g], in_sem.at[g])

    def put(g):
        return pltpu.make_async_copy(
            o_buf[g].at[pl.ds(0, PLACES)], out.at[:, pl.ds(SUM_FIRST[g], SUM_SIZES[g]), :], out_sem.at[g]
        )

    for g in range(PARTS):
        take(g).start()
    dens_copy.start()

    def clear(n, carry):
        for g in range(PARTS):
            o_buf[g][pl.ds(n * 4, 4)] = jnp.zeros((4, SUM_SIZES[g], TILE), jnp.float32)
        return carry

    lax.fori_loop(0, PLACES // 4, clear, 0)
    table_copy.wait()

    def compact(n, count):
        place = table[n]
        which[count] = n
        where[count] = place
        return count + (place >= 0).astype(jnp.int32)

    count = lax.fori_loop(0, DEV, compact, 0)
    for e in range(UNROLL - 1):
        which[count + e] = 0
        where[count + e] = PLACES
    rounds = (count + UNROLL - 1) // UNROLL

    for g in range(PARTS):
        take(g).wait()

        def add(m, carry, g=g):
            for e in range(UNROLL):
                o_buf[g][where[m * UNROLL + e]] += c_buf[g][which[m * UNROLL + e]].astype(jnp.float32)
            return carry

        lax.fori_loop(0, rounds, add, 0)
        put(g).start()
    for g in range(PARTS):
        put(g).wait()
    dens_copy.wait()


def scatter(table, dens, came):
    any_space = pl.BlockSpec(memory_space=pl.ANY)
    return pl.pallas_call(
        scatter_kernel,
        out_shape=(
            jax.ShapeDtypeStruct((PLACES, TILE, TILE), jnp.float32),
            jax.ShapeDtypeStruct((1, PTS), jnp.float32),
        ),
        in_specs=[any_space] * 3,
        out_specs=(any_space,) * 2,
        scratch_shapes=[
            pltpu.SMEM((DEV,), jnp.int32),
            [pltpu.VMEM((DEV, rows, TILE), jnp.bfloat16) for rows in SUM_SIZES],
            [pltpu.VMEM((PLACES + 1, rows, TILE), jnp.float32) for rows in SUM_SIZES],
            pltpu.SMEM((DEV + UNROLL,), jnp.int32),
            pltpu.SMEM((DEV + UNROLL,), jnp.int32),
            pltpu.SemaphoreType.DMA((PARTS,)),
            pltpu.SemaphoreType.DMA((PARTS,)),
            pltpu.SemaphoreType.DMA,
            pltpu.SemaphoreType.DMA,
        ],
        compiler_params=pltpu.CompilerParams(vmem_limit_bytes=60 * 2**20),
    )(table, dens, came)


def local(p_tiles, active, counts, basis, kernel):
    dens, came, table = exchange(
        active.T,
        counts,
        kernel,
        p_tiles.reshape(PLACES, TILE, TILE),
        basis.reshape(PTS, SPAN),
    )
    h_tiles, dens = scatter(table, dens, came)
    return h_tiles.reshape(p_tiles.shape), dens


def solution(mesh):
    return jax.shard_map(
        local,
        mesh=mesh,
        in_specs=(
            P(None, "row", None, "col", None, None),
            P(),
            P(("row", "col")),
            P(("row", "col"), None, None),
            P(("row", "col"), None),
        ),
        out_specs=(P(None, "row", None, "col", None, None), P(("row", "col"), None)),
        check_vma=False,
    )
```
